32 devices in a mesh: group: 2 (over y), expert: 8 (over z, core), tensor: 2 (over x).
Axes of the slice: x: 2, y: 2, z: 4, core: 2. Of those that a mesh axis runs over, the one named last changes fastest.
Arguments:
- tokens: bfloat16 [2048, 4096], P(('group', 'expert'), 'tensor'), parts along dimension 0, may hold values from -6 to 6
- expert_ids: int32 [2048, 4], P(('group', 'expert')), parts along dimension 0, may hold values from 0 to 7, all different within a row; in each aligned block of 128 rows (0 to 127, 128 to 255, ...) at most 96 rows name the same one
- gates: float32 [2048, 4], P(('group', 'expert')), parts along dimension 0, may hold values from 0.1 to 1
- gate_w: bfloat16 [8, 4096, 1536], P('expert', None, 'tensor'), may hold values from -0.09375 to 0.09375
- up_w: bfloat16 [8, 4096, 1536], P('expert', None, 'tensor'), may hold values from -0.09375 to 0.09375
- down_w: bfloat16 [8, 1536, 4096], P('expert', None, 'tensor'), may hold values from -0.15625 to 0.15625
Outputs:
- mixed: bfloat16 [2048, 4096], P(('group', 'expert'), 'tensor'), parts along dimension 0
The draws below stay inside these ranges and needn't reach their ends.
There are 2 independent parts, one for each index of `group`. The reference program is written for one: setup_inputs(seed, part) draws one part's arguments, and reference() takes and returns one part's arrays. A program takes and returns all parts, laid end to end along the dimension named above; an argument that names none is the same for every part. Nothing has to cross between parts.
Inputs may be any that keep to these rules, and one draw needn't show every extreme that they name: `expert_ids`: A row names 4 different experts. Among the rows of one index of the expert axis no expert is named by more than 96 rows, a bound that some block reaches of them.
All inputs are finite; a program needn't handle non-finite values.
Results may differ from the reference program's by a relative error of at most 0.0057.
Values may be sent and summed in bfloat16 or wider, within the bound.
A program may use at most 128 MiB of HBM per device.

```python
import math
import jax
import jax.numpy as jnp
import numpy as np
from jax import lax

D = 4096
H = 1536
TOP = 4
ROWS = 128
EXPERTS = 8
CAP = 96
ALL_ROWS = 1024
N_EXPERT = 8


def steps_of(own_key, shape, cuts, low, top_value):
    loudness, own = 1.0, jax.random.fold_in(own_key, 6)
    for position, blocks in cuts:
        draws = jnp.exp(jax.random.uniform(jax.random.fold_in(own, position), (blocks,), jnp.float32, low / len(cuts), top_value / len(cuts)))
        loudness = loudness * jnp.repeat(draws, shape[position] // blocks).reshape([-1 if axis == position else 1 for axis in range(len(shape))])
    return loudness


def shared_out(key, own, number, rows, amount, top, bound, lean):
    order = jax.random.permutation(key, amount)
    heavy_load, common = load_shares(amount, rows * top, bound, lean, True), load_shares(amount, rows * top, bound, lean, False)
    places = jnp.arange(amount)

    def named(lengths, rotation):
        used = int((lengths > 0).sum())
        fixed = max(1, used // 4)
        moved = fixed + (places - fixed + rotation * (used - fixed)) % max(1, amount - fixed)
        return jnp.zeros((amount,), jnp.int32).at[order[jnp.where(places < fixed, places, moved)]].set(jnp.asarray(lengths, jnp.int32))

    lengths = jnp.where(number % 4 == 0, named(heavy_load, number // 4), named(common, number - number // 4 - 1))
    mixed = jax.random.permutation(jax.random.fold_in(own, 3), amount)
    donor, sink = mixed[0:amount // 2 * 2:2], mixed[1:amount // 2 * 2:2]
    slack = jnp.minimum(lengths[donor] - 1, bound - lengths[sink]) // 2
    slack = jnp.where((donor == order[0]) | (sink == order[0]) | (lengths[sink] == 0), 0, jnp.maximum(slack, 0))
    moved = jax.random.randint(jax.random.fold_in(own, 4), (amount // 2,), 0, 1 << 20) % (slack + 1)
    lengths = lengths.at[donor].add(-moved).at[sink].add(moved)
    items = jnp.searchsorted(jnp.cumsum(lengths), jnp.arange(rows * top), side="right").astype(jnp.int32)
    table = items.reshape(top, rows).T
    table = table[jax.random.permutation(jax.random.fold_in(own, 1), rows)]
    rotation = jax.random.randint(jax.random.fold_in(own, 2), (rows, 1), 0, top)
    return jnp.take_along_axis(table, (jnp.arange(top)[None, :] + rotation) % top, axis=1)


def load_shares(number_of, total, limit, lean, full):
    loads = [(1 << 20) // math.isqrt(grade ** lean) + 1 for grade in range(1, number_of + 1)]
    largest = limit if full else min(limit, max(-(-total // number_of), total * loads[0] // sum(loads)))
    least = 1 if total - largest >= number_of - 1 else 0
    counts, surplus = [largest] + [least] * (number_of - 1), total - largest - least * (number_of - 1)
    while surplus > 0:
        candidates = [i for i in range(1, number_of) if counts[i] < largest] or [i for i in range(1, number_of) if counts[i] < limit]
        pool, budget = sum([loads[i] for i in candidates]), surplus
        for i in candidates:
            addition = min(limit - counts[i], max(1, budget * loads[i] // pool), surplus)
            counts[i] = counts[i] + addition
            surplus = surplus - addition
    return np.array(counts)


def bell_draw(key, extent, scale, limit, cuts=(), held_as=jnp.bfloat16):
    drawn = jax.random.normal(key, extent, jnp.float32) * scale
    if len(cuts) > 0:
        drawn = steps_of(key, extent, cuts, -0.22, 0.18) * drawn
    return jnp.clip(drawn, min=-limit, max=limit).astype(held_as)


def setup_inputs(seed: int = 0, part: int = 0) -> dict:
    keys = jax.random.split(jax.random.key(seed), 7)
    part_keys = jax.random.split(jax.random.fold_in(keys[6], part), 7)
    tokens = bell_draw(part_keys[0], (ALL_ROWS, D), 1.0, 6.0, ((0, 8), (1, 2)))
    expert_ids_keys = jax.random.split(jax.random.fold_in(part_keys[1], 1), ALL_ROWS // ROWS)
    expert_ids_turns = jax.random.permutation(jax.random.fold_in(part_keys[1], 3), ALL_ROWS // ROWS)
    expert_ids = jax.vmap(lambda own, number: shared_out(jax.random.fold_in(part_keys[1], 2), own, number, ROWS, EXPERTS, TOP, CAP, 2))(expert_ids_keys, expert_ids_turns).reshape((ALL_ROWS, TOP))
    gates = jnp.clip(jnp.exp(math.log(1.0) - 2.3025851 * jax.random.uniform(part_keys[2], (ALL_ROWS, TOP), jnp.float32) ** steps_of(part_keys[2], (ALL_ROWS, TOP), ((0, 8),), -0.2, 0.2)), 0.1, 1.0)
    gate_w = bell_draw(keys[3], (EXPERTS, D, H), D ** -0.5, 0.09375, ((0, 8), (2, 2)))
    up_w = bell_draw(keys[4], (EXPERTS, D, H), D ** -0.5, 0.09375, ((0, 8), (2, 2)))
    down_w = bell_draw(keys[5], (EXPERTS, H, D), H ** -0.5, 0.15625, ((0, 8), (2, 2)))
    return dict(tokens=tokens, expert_ids=expert_ids, gates=gates, gate_w=gate_w, up_w=up_w, down_w=down_w)


def expert_apply(rows_in, weight_gate, weight_up, weight_down):
    gate_part = jnp.dot(rows_in, weight_gate, preferred_element_type=jnp.float32)
    up_part = jnp.dot(rows_in, weight_up, preferred_element_type=jnp.float32)
    hidden = (jax.nn.silu(gate_part) * up_part).astype(jnp.bfloat16)
    return jnp.dot(hidden, weight_down, preferred_element_type=jnp.float32).astype(jnp.bfloat16)


def reference(tokens, expert_ids, gates, gate_w, up_w, down_w):
    flat_ids = expert_ids.reshape(-1).astype(jnp.int32)
    flat_gates = gates.reshape(-1)
    width = N_EXPERT * CAP

    def one_expert(index, total):
        index = jnp.asarray(index).astype(jnp.int32)
        matches = flat_ids == index
        found = jnp.nonzero(matches, size=width, fill_value=0)[0].astype(jnp.int32)
        howmany = jnp.sum(matches.astype(jnp.int32))
        valid = jnp.arange(width, dtype=jnp.int32) < howmany
        row_of = (found // TOP).astype(jnp.int32)
        picked = tokens[row_of]
        weight_gate = lax.dynamic_index_in_dim(gate_w, index, 0, keepdims=False)
        weight_up = lax.dynamic_index_in_dim(up_w, index, 0, keepdims=False)
        weight_down = lax.dynamic_index_in_dim(down_w, index, 0, keepdims=False)
        outputs = expert_apply(picked, weight_gate, weight_up, weight_down)
        scale = jnp.where(valid, flat_gates[found], jnp.zeros_like(flat_gates[found]))
        return total.at[row_of].add(scale[:, None] * outputs.astype(jnp.float32))

    start = jnp.zeros((tokens.shape[0], tokens.shape[1]), jnp.float32)
    total = lax.fori_loop(0, EXPERTS, one_expert, start)
    return total.astype(jnp.bfloat16)
```

```python
import jax
import jax.numpy as jnp
from jax import lax
from jax.sharding import PartitionSpec as P


def on_device(tokens, expert_ids, gates, gate_w, up_w, down_w):
    me = lax.axis_index("expert")
    whole = lax.all_gather(tokens, "tensor", axis=1, tiled=True)
    rows_all = lax.all_gather(whole, "expert", axis=0, tiled=True)
    peers = lax.axis_size("expert")
    own = jnp.sum(
        jnp.where(
            expert_ids[:, :, None] == jnp.arange(peers, dtype=jnp.int32)[None, None, :],
            gates[:, :, None],
            0.0,
        ),
        1,
    )
    weight = lax.dynamic_slice_in_dim(lax.all_gather(own, "expert", axis=0, tiled=True), me, 1, 1)
    gate_part = jnp.dot(rows_all, gate_w[0], preferred_element_type=jnp.float32)
    up_part = jnp.dot(rows_all, up_w[0], preferred_element_type=jnp.float32)
    hidden = (jax.nn.silu(gate_part) * up_part).astype(jnp.bfloat16)
    hidden = lax.all_gather(hidden, "tensor", axis=1, tiled=True)
    result = jnp.dot(hidden, down_w[0], preferred_element_type=jnp.float32)
    share = (result * weight).astype(jnp.bfloat16)
    return lax.psum_scatter(share, "expert", scatter_dimension=0, tiled=True)


def solution(mesh):
    in_specs = (
        P(("group", "expert"), "tensor"),
        P(("group", "expert"), None),
        P(("group", "expert"), None),
        P("expert", None, "tensor"),
        P("expert", None, "tensor"),
        P("expert", None, "tensor"),
    )
    out_specs = P(("group", "expert"), "tensor")
    return jax.shard_map(
        on_device, mesh=mesh, in_specs=in_specs, out_specs=out_specs, check_vma=False
    )
```

```python
import jax
import jax.numpy as jnp
from jax import lax
from jax.experimental import pallas as pl
from jax.experimental.pallas import tpu as pltpu
from jax.sharding import PartitionSpec as P


def dense(tokens, expert_ids, gates, gate_w, up_w, down_w):
    me = lax.axis_index("expert")
    whole = lax.all_gather(tokens, "tensor", axis=1, tiled=True)
    rows_all = lax.all_gather(whole, "expert", axis=0, tiled=True)
    peers = lax.axis_size("expert")
    own = jnp.sum(
        jnp.where(
            expert_ids[:, :, None] == jnp.arange(peers, dtype=jnp.int32)[None, None, :],
            gates[:, :, None],
            0.0,
        ),
        1,
    )
    weight = lax.dynamic_slice_in_dim(lax.all_gather(own, "expert", axis=0, tiled=True), me, 1, 1)
    gate_part = jnp.dot(rows_all, gate_w[0], preferred_element_type=jnp.float32)
    up_part = jnp.dot(rows_all, up_w[0], preferred_element_type=jnp.float32)
    hidden = (jax.nn.silu(gate_part) * up_part).astype(jnp.bfloat16)
    hidden = lax.all_gather(hidden, "tensor", axis=1, tiled=True)
    result = jnp.dot(hidden, down_w[0], preferred_element_type=jnp.float32)
    share = (result * weight).astype(jnp.bfloat16)
    return lax.psum_scatter(share, "expert", scatter_dimension=0, tiled=True)


MESH = pl.DeviceIdType.MESH
CHIPS = 4
TILE = 256
DOWN_TILE = 512


def kernel(
    tokens, own, gate_hbm, up_hbm, down_hbm, out,
    x_all, gate_w, up_w, down_w, hid, res, to_sib, from_sib, to_chip, from_chip, acc, wt,
    load_sem, z_send, x_send, s_send, w_send, h_send, r_send, c_send,
    z_recv, x_recv, s_recv, w_recv, h_recv, r_recv, c_recv,
):
    e = lax.axis_index("expert")
    x = lax.axis_index("tensor")
    z, c = lax.div(e, 2), lax.rem(e, 2)
    half = lax.div(z, 2)
    other = 1 - x
    x_peer = {"tensor": other}
    sibling = {"expert": z * 2 + 1 - c}
    rows = pl.ds(pl.multiple_of(c * 128, 128), 128)
    sib_rows = pl.ds(pl.multiple_of((1 - c) * 128, 128), 128)

    def chunk_of(s):
        near = z + (1 - 2 * z + 4 * half) * s
        far = 2 - half + (s - 2) * (1 - 2 * half)
        is_far = lax.div(s, 2)
        return near * (1 - is_far) + far * is_far

    def remote(src, dst, send, recv, device):
        return pltpu.make_async_remote_copy(
            src_ref=src, dst_ref=dst, send_sem=send, recv_sem=recv,
            device_id=device, device_id_type=MESH,
        )

    loads = [
        pltpu.make_async_copy(tokens, x_all.at[z, x, rows], load_sem.at[0]),
        pltpu.make_async_copy(gate_hbm, gate_w, load_sem.at[1]),
        pltpu.make_async_copy(up_hbm, up_w, load_sem.at[2]),
        pltpu.make_async_copy(down_hbm, down_w, load_sem.at[3]),
        pltpu.make_async_copy(own, wt.at[e], load_sem.at[4]),
    ]
    for load in (loads[0], loads[4], loads[1], loads[2], loads[3]):
        load.start()

    barrier = pltpu.get_barrier_semaphore()
    for d in range(1, 8):
        pl.semaphore_signal(
            barrier, inc=1, device_id={"expert": lax.rem(e + d, 8)}, device_id_type=MESH
        )
    pl.semaphore_signal(barrier, inc=1, device_id=x_peer, device_id_type=MESH)
    pl.semaphore_wait(barrier, 8)
    loads[0].wait()
    loads[4].wait()

    def piece(s, h):
        return x_all.at[chunk_of(s), h, rows]

    def to_right(s):
        q = chunk_of(s)
        return remote(piece(s, x), piece(s, x), z_send.at[s, 0], z_recv.at[q],
                      {"expert": lax.rem(e + 2, 8)})

    def to_left(s):
        q = chunk_of(s)
        return remote(piece(s, x), piece(s, x), z_send.at[s, 1], z_recv.at[q],
                      {"expert": lax.rem(e + 6, 8)})

    def across(s):
        return remote(piece(s, x), piece(s, x), x_send.at[s], x_recv.at[chunk_of(s)], x_peer)

    def beside(s, k):
        h = x if k == 0 else other
        return remote(piece(s, h), piece(s, h), s_send.at[s, k], s_recv.at[chunk_of(s), k], sibling)

    def weight(d):
        return remote(wt.at[e], wt.at[e], w_send.at[d], w_recv.at[e],
                      {"expert": lax.rem(e + d, 8)})

    def hidden_copy(s):
        q = chunk_of(s)
        return remote(hid.at[q, x], hid.at[q, x], h_send.at[s], h_recv.at[q], x_peer)

    def share_copy(s):
        return remote(to_sib.at[s], from_sib.at[s], r_send.at[s], r_recv.at[s], sibling)

    def chip_copy(s):
        return remote(to_chip.at[s], from_chip.at[z], c_send.at[s], c_recv.at[z],
                      {"expert": chunk_of(s) * 2 + c})

    def goes_right(s):
        return (chunk_of(s) <= z) & (z < CHIPS - 1)

    def goes_left(s):
        return (chunk_of(s) >= z) & (z > 0)

    def stage_a(s):
        q = chunk_of(s)

        @pl.when(s > 0)
        def _():
            remote(piece(s, x), piece(s, x), z_send.at[s, 0], z_recv.at[q], x_peer).wait_recv()

        @pl.when(goes_right(s))
        def _():
            to_right(s).start()

        @pl.when(goes_left(s))
        def _():
            to_left(s).start()

        across(s).start()
        beside(s, 0).start()

    def stage_b(s):
        q = chunk_of(s)
        remote(piece(s, other), piece(s, other), x_send.at[s], x_recv.at[q], x_peer).wait_recv()
        beside(s, 1).start()

    def stage_c(s):
        q = chunk_of(s)
        for k in range(2):
            h = x if k == 0 else other
            landed = x_all.at[q, h, sib_rows]
            remote(landed, landed, s_send.at[s, k], s_recv.at[q, k], sibling).wait_recv()

        @pl.loop(0, gate_w.shape[1] // TILE)
        def _(i):
            cols = pl.ds(pl.multiple_of(i * TILE, TILE), TILE)
            depth = x_all.shape[3]
            first, second = x_all[q, 0], x_all[q, 1]

            def both(w):
                return jnp.dot(
                    first, w[:depth, cols], preferred_element_type=jnp.float32
                ) + jnp.dot(second, w[depth:, cols], preferred_element_type=jnp.float32)

            g, u = both(gate_w), both(up_w)
            hid[q, x, :, cols] = (g / (1.0 + jnp.exp(-g)) * u).astype(jnp.bfloat16)

        hidden_copy(s).start()

    def stage_d(s):
        q = chunk_of(s)
        slot = lax.rem(s, 2)
        landed = hid.at[q, other]
        remote(landed, landed, h_send.at[s], h_recv.at[q], x_peer).wait_recv()
        eye = lax.broadcasted_iota(jnp.int32, (128, 128), 0) == lax.broadcasted_iota(
            jnp.int32, (128, 128), 1
        )

        def column(source):
            return jnp.sum(jnp.where(eye, wt[source, pl.ds(e, 1), :], 0.0), 1, keepdims=True)

        scale = jnp.concatenate([column(q * 2), column(q * 2 + 1)], 0)

        @pl.loop(0, down_w.shape[1] // DOWN_TILE)
        def _(i):
            cols = pl.ds(pl.multiple_of(i * DOWN_TILE, DOWN_TILE), DOWN_TILE)
            depth = hid.shape[3]
            part = jnp.dot(
                hid[q, 0], down_w[:depth, cols], preferred_element_type=jnp.float32
            ) + jnp.dot(hid[q, 1], down_w[depth:, cols], preferred_element_type=jnp.float32)
            res[slot, :, cols] = part * scale

        to_sib[s] = res[slot, sib_rows].astype(jnp.bfloat16)
        share_copy(s).start()

    def stage_e(s):
        slot = lax.rem(s, 2)
        share_copy(s).wait_recv()
        both = res[slot, rows] + from_sib[s].astype(jnp.float32)

        @pl.when(s == 0)
        def _():
            acc[...] = both

        @pl.when(s > 0)
        def _():
            to_chip[s] = both.astype(jnp.bfloat16)
            chip_copy(s).start()

    stage_a(jnp.int32(0))

    @pl.loop(1, 8)
    def _(d):
        weight(d).start()

    loads[1].wait()
    loads[2].wait()
    loads[3].wait()

    @pl.loop(1, 8)
    def _(d):
        source = lax.rem(e + d, 8)
        remote(wt.at[source], wt.at[source], w_send.at[d], w_recv.at[source], sibling).wait_recv()

    @pl.loop(0, CHIPS + 2)
    def _(t):
        @pl.when(t < CHIPS - 1)
        def _():
            stage_a(t + 1)

        @pl.when(t < CHIPS)
        def _():
            stage_b(t)
            stage_c(t)

        @pl.when((t >= 1) & (t < CHIPS + 1))
        def _():
            stage_d(t - 1)

        @pl.when(t >= 2)
        def _():
            stage_e(t - 2)

    @pl.loop(1, CHIPS)
    def _(s):
        q = chunk_of(s)
        remote(from_chip.at[q], from_chip.at[q], c_send.at[s], c_recv.at[q], sibling).wait_recv()
        acc[...] += from_chip[q].astype(jnp.float32)

    out[...] = acc[...].astype(jnp.bfloat16)

    @pl.loop(1, 8)
    def _(d):
        weight(d).wait_send()

    @pl.loop(0, CHIPS)
    def _(s):
        @pl.when(goes_right(s))
        def _():
            to_right(s).wait_send()

        @pl.when(goes_left(s))
        def _():
            to_left(s).wait_send()

        across(s).wait_send()
        beside(s, 0).wait_send()
        beside(s, 1).wait_send()
        hidden_copy(s).wait_send()
        share_copy(s).wait_send()

        @pl.when(s > 0)
        def _():
            chip_copy(s).wait_send()


def fused(tokens, expert_ids, gates, gate_w, up_w, down_w):
    rows, feats = tokens.shape
    hidden, width = gate_w.shape[2], down_w.shape[2]
    own = jnp.sum(
        jnp.where(
            expert_ids.T[None, :, :] == jnp.arange(8, dtype=jnp.int32)[:, None, None],
            gates.T[None, :, :],
            0.0,
        ),
        1,
    )
    dma = pltpu.SemaphoreType.DMA
    bf16, f32 = jnp.bfloat16, jnp.float32
    flops = 2 * 8 * rows * (2 * 2 * feats * hidden + 2 * hidden * width)
    return pl.pallas_call(
        kernel,
        out_shape=jax.ShapeDtypeStruct((rows, width), bf16),
        in_specs=[pl.BlockSpec(memory_space=pl.ANY)] * 5,
        out_specs=pl.BlockSpec(memory_space=pltpu.VMEM),
        scratch_shapes=[
            pltpu.VMEM((CHIPS, 2, 2 * rows, feats), bf16),
            pltpu.VMEM(gate_w.shape[1:], bf16),
            pltpu.VMEM(up_w.shape[1:], bf16),
            pltpu.VMEM(down_w.shape[1:], bf16),
            pltpu.VMEM((CHIPS, 2, 2 * rows, hidden), bf16),
            pltpu.VMEM((2, 2 * rows, width), f32),
            pltpu.VMEM((CHIPS, rows, width), bf16),
            pltpu.VMEM((CHIPS, rows, width), bf16),
            pltpu.VMEM((CHIPS, rows, width), bf16),
            pltpu.VMEM((CHIPS, rows, width), bf16),
            pltpu.VMEM((rows, width), f32),
            pltpu.VMEM((8, 8, rows), f32),
            dma((5,)), dma((4, 2)), dma((4,)), dma((4, 2)), dma((8,)), dma((4,)), dma((4,)), dma((4,)),
            dma((4,)), dma((4,)), dma((4, 2)), dma((8,)), dma((4,)), dma((4,)), dma((4,)),
        ],
        compiler_params=pltpu.CompilerParams(
            collective_id=0, has_side_effects=True, vmem_limit_bytes=56 * 1024 * 1024
        ),
        cost_estimate=pl.CostEstimate(flops=flops, bytes_accessed=20 << 20, transcendentals=1 << 20),
    )(tokens, own, gate_w[0], up_w[0], down_w[0])


def on_device(tokens, expert_ids, gates, gate_w, up_w, down_w):
    fits = (
        lax.axis_size("expert") == 8
        and lax.axis_size("tensor") == 2
        and tokens.shape == (128, 2048)
        and gate_w.shape[2] == 768
    )
    return (fused if fits else dense)(tokens, expert_ids, gates, gate_w, up_w, down_w)


def solution(mesh):
    in_specs = (
        P(("group", "expert"), "tensor"),
        P(("group", "expert"), None),
        P(("group", "expert"), None),
        P("expert", None, "tensor"),
        P("expert", None, "tensor"),
        P("expert", None, "tensor"),
    )
    out_specs = P(("group", "expert"), "tensor")
    return jax.shard_map(
        on_device, mesh=mesh, in_specs=in_specs, out_specs=out_specs, check_vma=False
    )
```

```python
import jax
import jax.numpy as jnp
from jax import lax
from jax.experimental import pallas as pl
from jax.experimental.pallas import tpu as pltpu
from jax.sharding import PartitionSpec as P


def dense(tokens, expert_ids, gates, gate_w, up_w, down_w):
    me = lax.axis_index("expert")
    whole = lax.all_gather(tokens, "tensor", axis=1, tiled=True)
    rows_all = lax.all_gather(whole, "expert", axis=0, tiled=True)
    peers = lax.axis_size("expert")
    own = jnp.sum(
        jnp.where(
            expert_ids[:, :, None] == jnp.arange(peers, dtype=jnp.int32)[None, None, :],
            gates[:, :, None],
            0.0,
        ),
        1,
    )
    weight = lax.dynamic_slice_in_dim(lax.all_gather(own, "expert", axis=0, tiled=True), me, 1, 1)
    gate_part = jnp.dot(rows_all, gate_w[0], preferred_element_type=jnp.float32)
    up_part = jnp.dot(rows_all, up_w[0], preferred_element_type=jnp.float32)
    hidden = (jax.nn.silu(gate_part) * up_part).astype(jnp.bfloat16)
    hidden = lax.all_gather(hidden, "tensor", axis=1, tiled=True)
    result = jnp.dot(hidden, down_w[0], preferred_element_type=jnp.float32)
    share = (result * weight).astype(jnp.bfloat16)
    return lax.psum_scatter(share, "expert", scatter_dimension=0, tiled=True)


MESH = pl.DeviceIdType.MESH
CHIPS = 4
TILE = 256
DOWN_TILE = 512
ALONG = 512


def kernel(
    tokens, own, gate_hbm, up_hbm, down_hbm, out,
    x_all, gate_w, up_w, down_w, hid, res, to_sib, from_sib, to_chip, from_chip, acc, wt,
    load_sem, z_send, n_send, x_send, s_send, w_send, h_send, r_send, c_send,
    z_recv, n_recv, x_recv, s_recv, w_recv, h_recv, r_recv, c_recv,
):
    e = lax.axis_index("expert")
    x = lax.axis_index("tensor")
    z, c = lax.div(e, 2), lax.rem(e, 2)
    half = lax.div(z, 2)
    other = 1 - x
    x_peer = {"tensor": other}
    sibling = {"expert": z * 2 + 1 - c}
    rows = pl.ds(pl.multiple_of(c * 128, 128), 128)
    sib_rows = pl.ds(pl.multiple_of((1 - c) * 128, 128), 128)

    def chunk_of(s):
        near = z + (1 - 2 * z + 4 * half) * s
        far = 2 - half + (s - 2) * (1 - 2 * half)
        is_far = lax.div(s, 2)
        return near * (1 - is_far) + far * is_far

    def remote(src, dst, send, recv, device):
        return pltpu.make_async_remote_copy(
            src_ref=src, dst_ref=dst, send_sem=send, recv_sem=recv,
            device_id=device, device_id_type=MESH,
        )

    loads = [
        pltpu.make_async_copy(tokens, x_all.at[z, x, rows], load_sem.at[0]),
        pltpu.make_async_copy(gate_hbm, gate_w, load_sem.at[1]),
        pltpu.make_async_copy(up_hbm, up_w, load_sem.at[2]),
        pltpu.make_async_copy(down_hbm, down_w, load_sem.at[3]),
        pltpu.make_async_copy(own, wt.at[e], load_sem.at[4]),
    ]
    for load in (loads[0], loads[4], loads[1], loads[2], loads[3]):
        load.start()

    barrier = pltpu.get_barrier_semaphore()
    for d in range(1, 8):
        pl.semaphore_signal(
            barrier, inc=1, device_id={"expert": lax.rem(e + d, 8)}, device_id_type=MESH
        )
    pl.semaphore_signal(barrier, inc=1, device_id=x_peer, device_id_type=MESH)
    pl.semaphore_wait(barrier, 8)
    loads[0].wait()
    loads[4].wait()

    def piece(s, h):
        return x_all.at[chunk_of(s), h, rows]

    def to_right(s):
        q = chunk_of(s)
        return remote(piece(s, x), piece(s, x), z_send.at[s, 0], z_recv.at[q],
                      {"expert": lax.rem(e + 2, 8)})

    def to_left(s):
        q = chunk_of(s)
        return remote(piece(s, x), piece(s, x), z_send.at[s, 1], z_recv.at[q],
                      {"expert": lax.rem(e + 6, 8)})

    def along(s):
        return x_all.at[chunk_of(s), other, rows, pl.ds(0, ALONG)]

    def along_to(s, side):
        return remote(along(s), along(s), n_send.at[s, side], n_recv.at[chunk_of(s)],
                      {"expert": lax.rem(e + (2 if side == 0 else 6), 8)})

    def across_own():
        return remote(piece(0, x), piece(0, x), x_send.at[0], x_recv.at[z], x_peer)

    def across(s, h):
        q = chunk_of(s)
        part = x_all.at[q, h, rows, pl.ds(ALONG, x_all.shape[3] - ALONG)]
        return remote(part, part, x_send.at[s], x_recv.at[q], x_peer)

    def beside(s, k):
        h = x if k == 0 else other
        return remote(piece(s, h), piece(s, h), s_send.at[s, k], s_recv.at[chunk_of(s), k], sibling)

    def weight(d):
        return remote(wt.at[e], wt.at[e], w_send.at[d], w_recv.at[e],
                      {"expert": lax.rem(e + d, 8)})

    def hidden_copy(s):
        q = chunk_of(s)
        return remote(hid.at[q, x], hid.at[q, x], h_send.at[s], h_recv.at[q], x_peer)

    def share_copy(s):
        return remote(to_sib.at[s], from_sib.at[s], r_send.at[s], r_recv.at[s], sibling)

    def chip_copy(s):
        return remote(to_chip.at[s], from_chip.at[z], c_send.at[s], c_recv.at[z],
                      {"expert": chunk_of(s) * 2 + c})

    def goes_right(s):
        return (chunk_of(s) <= z) & (z < CHIPS - 1)

    def goes_left(s):
        return (chunk_of(s) >= z) & (z > 0)

    def stage_a(s):
        q = chunk_of(s)

        @pl.when(s > 0)
        def _():
            remote(piece(s, x), piece(s, x), z_send.at[s, 0], z_recv.at[q], x_peer).wait_recv()

        @pl.when(goes_right(s))
        def _():
            to_right(s).start()

        @pl.when(goes_left(s))
        def _():
            to_left(s).start()

        @pl.when(s == 0)
        def _():
            across_own().start()

        @pl.when(s > 0)
        def _():
            across(s, x).start()

        beside(s, 0).start()

    def stage_b(s):
        @pl.when(s == 0)
        def _():
            mine = piece(0, other)
            remote(mine, mine, x_send.at[0], x_recv.at[z], x_peer).wait_recv()

        @pl.when(s > 0)
        def _():
            remote(along(s), along(s), n_send.at[s, 0], n_recv.at[chunk_of(s)], x_peer).wait_recv()

        @pl.when(goes_right(s))
        def _():
            along_to(s, 0).start()

        @pl.when(goes_left(s))
        def _():
            along_to(s, 1).start()

        @pl.when(s > 0)
        def _():
            across(s, other).wait_recv()

        beside(s, 1).start()

    def stage_c(s):
        q = chunk_of(s)
        for k in range(2):
            h = x if k == 0 else other
            landed = x_all.at[q, h, sib_rows]
            remote(landed, landed, s_send.at[s, k], s_recv.at[q, k], sibling).wait_recv()

        @pl.loop(0, gate_w.shape[1] // TILE)
        def _(i):
            cols = pl.ds(pl.multiple_of(i * TILE, TILE), TILE)
            depth = x_all.shape[3]
            first, second = x_all[q, 0], x_all[q, 1]

            def both(w):
                return jnp.dot(
                    first, w[:depth, cols], preferred_element_type=jnp.float32
                ) + jnp.dot(second, w[depth:, cols], preferred_element_type=jnp.float32)

            g, u = both(gate_w), both(up_w)
            hid[q, x, :, cols] = (g / (1.0 + jnp.exp(-g)) * u).astype(jnp.bfloat16)

    def stage_d(s, slot):
        q = chunk_of(s)
        landed = hid.at[q, other]
        remote(landed, landed, h_send.at[s], h_recv.at[q], x_peer).wait_recv()
        eye = lax.broadcasted_iota(jnp.int32, (128, 128), 0) == lax.broadcasted_iota(
            jnp.int32, (128, 128), 1
        )

        def column(source):
            return jnp.sum(jnp.where(eye, wt[source, pl.ds(e, 1), :], 0.0), 1, keepdims=True)

        scale = jnp.concatenate([column(q * 2), column(q * 2 + 1)], 0)

        @pl.loop(0, down_w.shape[1] // DOWN_TILE)
        def _(i):
            cols = pl.ds(pl.multiple_of(i * DOWN_TILE, DOWN_TILE), DOWN_TILE)
            depth = hid.shape[3]
            part = jnp.dot(
                hid[q, 0], down_w[:depth, cols], preferred_element_type=jnp.float32
            ) + jnp.dot(hid[q, 1], down_w[depth:, cols], preferred_element_type=jnp.float32)
            res[slot, :, cols] = part * scale

        to_sib[s] = res[slot, sib_rows].astype(jnp.bfloat16)
        share_copy(s).start()

    def stage_e(s, slot):
        share_copy(s).wait_recv()
        both = res[slot, rows] + from_sib[s].astype(jnp.float32)

        @pl.when(s == 0)
        def _():
            acc[...] = both

        @pl.when(s > 0)
        def _():
            to_chip[s] = both.astype(jnp.bfloat16)
            chip_copy(s).start()

    stage_a(jnp.int32(0))

    @pl.loop(1, 8)
    def _(d):
        weight(d).start()

    loads[1].wait()
    loads[2].wait()
    loads[3].wait()

    @pl.loop(1, 8)
    def _(d):
        source = lax.rem(e + d, 8)
        remote(wt.at[source], wt.at[source], w_send.at[d], w_recv.at[source], sibling).wait_recv()

    @pl.loop(0, CHIPS)
    def _(t):
        @pl.when(t < CHIPS - 1)
        def _():
            stage_a(t + 1)

        stage_b(t)
        stage_c(t)

        @pl.when(t >= 2)
        def _():
            hidden_copy(t).start()

        @pl.when(t == CHIPS - 1)
        def _():
            hidden_copy(jnp.int32(1)).start()
            hidden_copy(jnp.int32(0)).start()

    def turn(u):
        late = lax.div(u, 2)
        return (u + 2) * (1 - late) + (3 - u) * late

    @pl.loop(0, CHIPS + 1)
    def _(u):
        @pl.when(u < CHIPS)
        def _():
            stage_d(turn(u), lax.rem(u, 2))

        @pl.when(u > 0)
        def _():
            stage_e(turn(u - 1), lax.rem(u - 1, 2))

    @pl.loop(1, CHIPS)
    def _(s):
        q = chunk_of(s)
        remote(from_chip.at[q], from_chip.at[q], c_send.at[s], c_recv.at[q], sibling).wait_recv()
        acc[...] += from_chip[q].astype(jnp.float32)

    out[...] = acc[...].astype(jnp.bfloat16)

    @pl.loop(1, 8)
    def _(d):
        weight(d).wait_send()

    @pl.loop(0, CHIPS)
    def _(s):
        @pl.when(goes_right(s))
        def _():
            to_right(s).wait_send()
            along_to(s, 0).wait_send()

        @pl.when(goes_left(s))
        def _():
            to_left(s).wait_send()
            along_to(s, 1).wait_send()

        @pl.when(s == 0)
        def _():
            across_own().wait_send()

        @pl.when(s > 0)
        def _():
            across(s, x).wait_send()

        beside(s, 0).wait_send()
        beside(s, 1).wait_send()
        hidden_copy(s).wait_send()
        share_copy(s).wait_send()

        @pl.when(s > 0)
        def _():
            chip_copy(s).wait_send()


def fused(tokens, expert_ids, gates, gate_w, up_w, down_w):
    rows, feats = tokens.shape
    hidden, width = gate_w.shape[2], down_w.shape[2]
    own = jnp.sum(
        jnp.where(
            expert_ids.T[None, :, :] == jnp.arange(8, dtype=jnp.int32)[:, None, None],
            gates.T[None, :, :],
            0.0,
        ),
        1,
    )
    dma = pltpu.SemaphoreType.DMA
    bf16, f32 = jnp.bfloat16, jnp.float32
    flops = 2 * 8 * rows * (2 * 2 * feats * hidden + 2 * hidden * width)
    return pl.pallas_call(
        kernel,
        out_shape=jax.ShapeDtypeStruct((rows, width), bf16),
        in_specs=[pl.BlockSpec(memory_space=pl.ANY)] * 5,
        out_specs=pl.BlockSpec(memory_space=pltpu.VMEM),
        scratch_shapes=[
            pltpu.VMEM((CHIPS, 2, 2 * rows, feats), bf16),
            pltpu.VMEM(gate_w.shape[1:], bf16),
            pltpu.VMEM(up_w.shape[1:], bf16),
            pltpu.VMEM(down_w.shape[1:], bf16),
            pltpu.VMEM((CHIPS, 2, 2 * rows, hidden), bf16),
            pltpu.VMEM((2, 2 * rows, width), f32),
            pltpu.VMEM((CHIPS, rows, width), bf16),
            pltpu.VMEM((CHIPS, rows, width), bf16),
            pltpu.VMEM((CHIPS, rows, width), bf16),
            pltpu.VMEM((CHIPS, rows, width), bf16),
            pltpu.VMEM((rows, width), f32),
            pltpu.VMEM((8, 8, rows), f32),
            dma((5,)), dma((4, 2)), dma((4, 2)), dma((4,)), dma((4, 2)), dma((8,)), dma((4,)), dma((4,)), dma((4,)),
            dma((4,)), dma((4,)), dma((4,)), dma((4, 2)), dma((8,)), dma((4,)), dma((4,)), dma((4,)),
        ],
        compiler_params=pltpu.CompilerParams(
            collective_id=0, has_side_effects=True, vmem_limit_bytes=56 * 1024 * 1024
        ),
        cost_estimate=pl.CostEstimate(flops=flops, bytes_accessed=20 << 20, transcendentals=1 << 20),
    )(tokens, own, gate_w[0], up_w[0], down_w[0])


def on_device(tokens, expert_ids, gates, gate_w, up_w, down_w):
    fits = (
        lax.axis_size("expert") == 8
        and lax.axis_size("tensor") == 2
        and tokens.shape == (128, 2048)
        and gate_w.shape[2] == 768
    )
    return (fused if fits else dense)(tokens, expert_ids, gates, gate_w, up_w, down_w)


def solution(mesh):
    in_specs = (
        P(("group", "expert"), "tensor"),
        P(("group", "expert"), None),
        P(("group", "expert"), None),
        P("expert", None, "tensor"),
        P("expert", None, "tensor"),
        P("expert", None, "tensor"),
    )
    out_specs = P(("group", "expert"), "tensor")
    return jax.shard_map(
        on_device, mesh=mesh, in_specs=in_specs, out_specs=out_specs, check_vma=False
    )
```

```python
import jax
import jax.numpy as jnp
from jax import lax
from jax.experimental import pallas as pl
from jax.experimental.pallas import tpu as pltpu
from jax.sharding import PartitionSpec as P


def dense(tokens, expert_ids, gates, gate_w, up_w, down_w):
    me = lax.axis_index("expert")
    whole = lax.all_gather(tokens, "tensor", axis=1, tiled=True)
    rows_all = lax.all_gather(whole, "expert", axis=0, tiled=True)
    peers = lax.axis_size("expert")
    own = jnp.sum(
        jnp.where(
            expert_ids[:, :, None] == jnp.arange(peers, dtype=jnp.int32)[None, None, :],
            gates[:, :, None],
            0.0,
        ),
        1,
    )
    weight = lax.dynamic_slice_in_dim(lax.all_gather(own, "expert", axis=0, tiled=True), me, 1, 1)
    gate_part = jnp.dot(rows_all, gate_w[0], preferred_element_type=jnp.float32)
    up_part = jnp.dot(rows_all, up_w[0], preferred_element_type=jnp.float32)
    hidden = (jax.nn.silu(gate_part) * up_part).astype(jnp.bfloat16)
    hidden = lax.all_gather(hidden, "tensor", axis=1, tiled=True)
    result = jnp.dot(hidden, down_w[0], preferred_element_type=jnp.float32)
    share = (result * weight).astype(jnp.bfloat16)
    return lax.psum_scatter(share, "expert", scatter_dimension=0, tiled=True)


MESH = pl.DeviceIdType.MESH
CHIPS = 4
TILE = 256
DOWN_TILE = 512
ALONG = 512


def kernel(
    tokens, own, gate_hbm, up_hbm, down_hbm, out,
    x_all, gate_w, up_w, down_w, hid, res, to_sib, from_sib, to_chip, from_chip, acc, wt,
    load_sem, z_send, n_send, x_send, s_send, w_send, h_send, r_send, c_send,
    z_recv, n_recv, x_recv, s_recv, w_recv, h_recv, r_recv, c_recv,
):
    e = lax.axis_index("expert")
    x = lax.axis_index("tensor")
    z, c = lax.div(e, 2), lax.rem(e, 2)
    half = lax.div(z, 2)
    other = 1 - x
    x_peer = {"tensor": other}
    sibling = {"expert": z * 2 + 1 - c}
    rows = pl.ds(pl.multiple_of(c * 128, 128), 128)
    sib_rows = pl.ds(pl.multiple_of((1 - c) * 128, 128), 128)

    def chunk_of(s):
        near = z + (1 - 2 * z + 4 * half) * s
        far = 2 - half + (s - 2) * (1 - 2 * half)
        is_far = lax.div(s, 2)
        return near * (1 - is_far) + far * is_far

    def remote(src, dst, send, recv, device):
        return pltpu.make_async_remote_copy(
            src_ref=src, dst_ref=dst, send_sem=send, recv_sem=recv,
            device_id=device, device_id_type=MESH,
        )

    loads = [
        pltpu.make_async_copy(tokens, x_all.at[z, x, rows], load_sem.at[0]),
        pltpu.make_async_copy(gate_hbm, gate_w, load_sem.at[1]),
        pltpu.make_async_copy(up_hbm, up_w, load_sem.at[2]),
        pltpu.make_async_copy(down_hbm, down_w, load_sem.at[3]),
        pltpu.make_async_copy(own, wt.at[e], load_sem.at[4]),
    ]
    for load in (loads[0], loads[4], loads[1], loads[2], loads[3]):
        load.start()

    barrier = pltpu.get_barrier_semaphore()
    for d in range(1, 8):
        pl.semaphore_signal(
            barrier, inc=1, device_id={"expert": lax.rem(e + d, 8)}, device_id_type=MESH
        )
    pl.semaphore_signal(barrier, inc=1, device_id=x_peer, device_id_type=MESH)
    pl.semaphore_wait(barrier, 8)
    loads[0].wait()
    loads[4].wait()

    def piece(s, h):
        return x_all.at[chunk_of(s), h, rows]

    def to_right(s):
        q = chunk_of(s)
        return remote(piece(s, x), piece(s, x), z_send.at[s, 0], z_recv.at[q],
                      {"expert": lax.rem(e + 2, 8)})

    def to_left(s):
        q = chunk_of(s)
        return remote(piece(s, x), piece(s, x), z_send.at[s, 1], z_recv.at[q],
                      {"expert": lax.rem(e + 6, 8)})

    def along(s):
        return x_all.at[chunk_of(s), other, rows, pl.ds(0, ALONG)]

    def along_to(s, side):
        return remote(along(s), along(s), n_send.at[s, side], n_recv.at[chunk_of(s)],
                      {"expert": lax.rem(e + (2 if side == 0 else 6), 8)})

    def across_own():
        return remote(piece(0, x), piece(0, x), x_send.at[0], x_recv.at[z], x_peer)

    def across(s, h):
        q = chunk_of(s)
        part = x_all.at[q, h, rows, pl.ds(ALONG, x_all.shape[3] - ALONG)]
        return remote(part, part, x_send.at[s], x_recv.at[q], x_peer)

    def beside(s, k):
        h = x if k == 0 else other
        return remote(piece(s, h), piece(s, h), s_send.at[s, k], s_recv.at[chunk_of(s), k], sibling)

    def weight(d):
        return remote(wt.at[e], wt.at[e], w_send.at[d], w_recv.at[e],
                      {"expert": lax.rem(e + d, 8)})

    def hidden_copy(s):
        q = chunk_of(s)
        return remote(hid.at[q, x], hid.at[q, x], h_send.at[s], h_recv.at[q], x_peer)

    def share_copy(s):
        return remote(to_sib.at[s], from_sib.at[s], r_send.at[s], r_recv.at[s], sibling)

    def chip_copy(s):
        return remote(to_chip.at[s], from_chip.at[z], c_send.at[s], c_recv.at[z],
                      {"expert": chunk_of(s) * 2 + c})

    def goes_right(s):
        return (chunk_of(s) <= z) & (z < CHIPS - 1)

    def goes_left(s):
        return (chunk_of(s) >= z) & (z > 0)

    def stage_a(s):
        q = chunk_of(s)

        @pl.when(s > 0)
        def _():
            remote(piece(s, x), piece(s, x), z_send.at[s, 0], z_recv.at[q], x_peer).wait_recv()

        @pl.when(goes_right(s))
        def _():
            to_right(s).start()

        @pl.when(goes_left(s))
        def _():
            to_left(s).start()

        @pl.when(s == 0)
        def _():
            across_own().start()

        @pl.when(s > 0)
        def _():
            across(s, x).start()

        beside(s, 0).start()

    def stage_b(s):
        @pl.when(s == 0)
        def _():
            mine = piece(0, other)
            remote(mine, mine, x_send.at[0], x_recv.at[z], x_peer).wait_recv()

        @pl.when(s > 0)
        def _():
            remote(along(s), along(s), n_send.at[s, 0], n_recv.at[chunk_of(s)], x_peer).wait_recv()

        @pl.when(goes_right(s))
        def _():
            along_to(s, 0).start()

        @pl.when(goes_left(s))
        def _():
            along_to(s, 1).start()

        @pl.when(s > 0)
        def _():
            across(s, other).wait_recv()

        beside(s, 1).start()

    def stage_c(s):
        q = chunk_of(s)
        for k in range(2):
            h = x if k == 0 else other
            landed = x_all.at[q, h, sib_rows]
            remote(landed, landed, s_send.at[s, k], s_recv.at[q, k], sibling).wait_recv()

        @pl.loop(0, gate_w.shape[1] // TILE)
        def _(i):
            cols = pl.ds(pl.multiple_of(i * TILE, TILE), TILE)
            depth = x_all.shape[3]
            first, second = x_all[q, 0], x_all[q, 1]

            def both(w):
                return jnp.dot(
                    first, w[:depth, cols], preferred_element_type=jnp.float32
                ) + jnp.dot(second, w[depth:, cols], preferred_element_type=jnp.float32)

            g, u = both(gate_w), both(up_w)
            hid[q, x, :, cols] = (g / (1.0 + jnp.exp(-g)) * u).astype(jnp.bfloat16)

    def stage_d(s, slot):
        q = chunk_of(s)
        landed = hid.at[q, other]
        remote(landed, landed, h_send.at[s], h_recv.at[q], x_peer).wait_recv()
        eye = lax.broadcasted_iota(jnp.int32, (128, 128), 0) == lax.broadcasted_iota(
            jnp.int32, (128, 128), 1
        )

        def column(source):
            return jnp.sum(jnp.where(eye, wt[source, pl.ds(e, 1), :], 0.0), 1, keepdims=True)

        scale = jnp.concatenate([column(q * 2), column(q * 2 + 1)], 0)

        @pl.loop(0, down_w.shape[1] // DOWN_TILE)
        def _(i):
            cols = pl.ds(pl.multiple_of(i * DOWN_TILE, DOWN_TILE), DOWN_TILE)
            depth = hid.shape[3]
            part = jnp.dot(
                hid[q, 0], down_w[:depth, cols], preferred_element_type=jnp.float32
            ) + jnp.dot(hid[q, 1], down_w[depth:, cols], preferred_element_type=jnp.float32)
            res[slot, :, cols] = part * scale

        to_sib[s] = res[slot, sib_rows].astype(jnp.bfloat16)
        share_copy(s).start()

    def stage_e(s, slot):
        share_copy(s).wait_recv()
        both = res[slot, rows] + from_sib[s].astype(jnp.float32)

        @pl.when(s == 0)
        def _():
            acc[...] = both

        @pl.when(s > 0)
        def _():
            to_chip[s] = both.astype(jnp.bfloat16)
            chip_copy(s).start()

    stage_a(jnp.int32(0))

    @pl.loop(1, 8)
    def _(d):
        weight(d).start()

    loads[1].wait()
    loads[2].wait()
    loads[3].wait()

    @pl.loop(1, 8)
    def _(d):
        source = lax.rem(e + d, 8)
        remote(wt.at[source], wt.at[source], w_send.at[d], w_recv.at[source], sibling).wait_recv()

    @pl.loop(0, CHIPS)
    def _(t):
        @pl.when(t < CHIPS - 1)
        def _():
            stage_a(t + 1)

        stage_b(t)
        stage_c(t)

        @pl.when(t >= 2)
        def _():
            hidden_copy(t).start()

        @pl.when(t == CHIPS - 1)
        def _():
            hidden_copy(jnp.int32(1)).start()
            hidden_copy(jnp.int32(0)).start()

    def turn(u):
        late = lax.div(u, 2)
        return (u + 2) * (1 - late) + (3 - u) * late

    @pl.loop(0, CHIPS)
    def _(u):
        stage_d(turn(u), lax.rem(u, 2))
        stage_e(turn(u), lax.rem(u, 2))

    @pl.loop(1, CHIPS)
    def _(s):
        q = chunk_of(s)
        remote(from_chip.at[q], from_chip.at[q], c_send.at[s], c_recv.at[q], sibling).wait_recv()
        acc[...] += from_chip[q].astype(jnp.float32)

    out[...] = acc[...].astype(jnp.bfloat16)

    @pl.loop(1, 8)
    def _(d):
        weight(d).wait_send()

    @pl.loop(0, CHIPS)
    def _(s):
        @pl.when(goes_right(s))
        def _():
            to_right(s).wait_send()
            along_to(s, 0).wait_send()

        @pl.when(goes_left(s))
        def _():
            to_left(s).wait_send()
            along_to(s, 1).wait_send()

        @pl.when(s == 0)
        def _():
            across_own().wait_send()

        @pl.when(s > 0)
        def _():
            across(s, x).wait_send()

        beside(s, 0).wait_send()
        beside(s, 1).wait_send()
        hidden_copy(s).wait_send()
        share_copy(s).wait_send()

        @pl.when(s > 0)
        def _():
            chip_copy(s).wait_send()


def fused(tokens, expert_ids, gates, gate_w, up_w, down_w):
    rows, feats = tokens.shape
    hidden, width = gate_w.shape[2], down_w.shape[2]
    own = jnp.sum(
        jnp.where(
            expert_ids.T[None, :, :] == jnp.arange(8, dtype=jnp.int32)[:, None, None],
            gates.T[None, :, :],
            0.0,
        ),
        1,
    )
    dma = pltpu.SemaphoreType.DMA
    bf16, f32 = jnp.bfloat16, jnp.float32
    flops = 2 * 8 * rows * (2 * 2 * feats * hidden + 2 * hidden * width)
    return pl.pallas_call(
        kernel,
        out_shape=jax.ShapeDtypeStruct((rows, width), bf16),
        in_specs=[pl.BlockSpec(memory_space=pl.ANY)] * 5,
        out_specs=pl.BlockSpec(memory_space=pltpu.VMEM),
        scratch_shapes=[
            pltpu.VMEM((CHIPS, 2, 2 * rows, feats), bf16),
            pltpu.VMEM(gate_w.shape[1:], bf16),
            pltpu.VMEM(up_w.shape[1:], bf16),
            pltpu.VMEM(down_w.shape[1:], bf16),
            pltpu.VMEM((CHIPS, 2, 2 * rows, hidden), bf16),
            pltpu.VMEM((2, 2 * rows, width), f32),
            pltpu.VMEM((CHIPS, rows, width), bf16),
            pltpu.VMEM((CHIPS, rows, width), bf16),
            pltpu.VMEM((CHIPS, rows, width), bf16),
            pltpu.VMEM((CHIPS, rows, width), bf16),
            pltpu.VMEM((rows, width), f32),
            pltpu.VMEM((8, 8, rows), f32),
            dma((5,)), dma((4, 2)), dma((4, 2)), dma((4,)), dma((4, 2)), dma((8,)), dma((4,)), dma((4,)), dma((4,)),
            dma((4,)), dma((4,)), dma((4,)), dma((4, 2)), dma((8,)), dma((4,)), dma((4,)), dma((4,)),
        ],
        compiler_params=pltpu.CompilerParams(
            collective_id=0, has_side_effects=True, vmem_limit_bytes=56 * 1024 * 1024
        ),
        cost_estimate=pl.CostEstimate(flops=flops, bytes_accessed=20 << 20, transcendentals=1 << 20),
    )(tokens, own, gate_w[0], up_w[0], down_w[0])


def on_device(tokens, expert_ids, gates, gate_w, up_w, down_w):
    fits = (
        lax.axis_size("expert") == 8
        and lax.axis_size("tensor") == 2
        and tokens.shape == (128, 2048)
        and gate_w.shape[2] == 768
    )
    return (fused if fits else dense)(tokens, expert_ids, gates, gate_w, up_w, down_w)


def solution(mesh):
    in_specs = (
        P(("group", "expert"), "tensor"),
        P(("group", "expert"), None),
        P(("group", "expert"), None),
        P("expert", None, "tensor"),
        P("expert", None, "tensor"),
        P("expert", None, "tensor"),
    )
    out_specs = P(("group", "expert"), "tensor")
    return jax.shard_map(
        on_device, mesh=mesh, in_specs=in_specs, out_specs=out_specs, check_vma=False
    )
```
